32 devices in a mesh: gx: 8 (over z, core), gy: 4 (over y, x).
Axes of the slice: x: 2, y: 2, z: 4, core: 2. Of those that a mesh axis runs over, the one named last changes fastest.
Arguments:
- bottom_in: bfloat16 [8192, 256], P(('gx', 'gy')), may hold values from -6 to 6
- bottom_pre: bfloat16 [8192, 128], P(('gx', 'gy')), may hold values from -6 to 6
- pooled: bfloat16 [8192, 2, 128], P(('gx', 'gy')), may hold values from -6 to 6
- top_pre: bfloat16 [8192, 1024], P(('gx', 'gy')), may hold values from -6 to 6
- top_cotangent: bfloat16 [8192, 1024], P(('gx', 'gy')), may hold values from -0.375 to 0.375
- top_weight: bfloat16 [384, 1024], replicated, may hold values from -0.5 to 0.5
- lookup_owner: int32 [8192, 2, 32], P(('gx', 'gy')), may hold values from 0 to 31, as said below
- lookup_row: int32 [8192, 2, 32], P(('gx', 'gy')), may hold values from 0 to 2047
Outputs:
- table_grad: float32 [2, 65536, 128], P(None, ('gx', 'gy'))
- top_weight_grad: float32 [384, 1024], P('gy')
- top_bias_grad: float32 [1024], P('gy')
- bottom_weight_grad: float32 [256, 128], P('gy')
The draws below stay inside these ranges and needn't reach their ends.
Inputs may be any that keep to these rules, and one draw needn't show every extreme that they name: `lookup_owner`: row r of a table with r = owner * 2048 + row is held by device owner in the order of gx+gy. Among the lookups of one device's 256 bags and one table, every owner number appears at most 512 times, and one owner number, the same for all devices of that table, exactly 512 times.
All inputs are finite; a program needn't handle non-finite values.
Results may differ from the reference program's by a relative error of at most 0.003.
Values may be sent and summed in bfloat16 or wider, within the bound.
A program may use at most 128 MiB of HBM per device.

```python
import math
import jax
import jax.numpy as jnp
import numpy as np
from jax import lax

D = 128
TOP = 1024
BOT_IN = 256
TABLES = 2
BAG = 32
ROWS_DEV = 2048
B_DEV = 256
BATCH = 8192
ROWS = 65536
TOP_IN = 384
CAP = 512
DEVICES = 32


def draw_lookup_owner(key, part):
    hot_key = jax.random.fold_in(key, 11)
    mix_key = jax.random.fold_in(key, 23)
    hot_owner = jax.random.randint(hot_key, (TABLES,), 0, DEVICES)
    spread = B_DEV * BAG - CAP
    others_base = jnp.repeat(jnp.arange(1, DEVICES, dtype=jnp.int32), CAP)

    def one_list(inner_key, hot_value):
        first_key = jax.random.fold_in(inner_key, 1)
        second_key = jax.random.fold_in(inner_key, 2)
        chosen = jax.random.permutation(first_key, others_base)[:spread]
        listed = jnp.concatenate([jnp.zeros((CAP,), jnp.int32), chosen.astype(jnp.int32)])
        listed = jax.random.permutation(second_key, listed)
        return (listed + hot_value) % DEVICES
    list_keys = jax.random.split(mix_key, DEVICES * TABLES)
    hot_all = jnp.tile(hot_owner, DEVICES)
    drawn = jax.vmap(one_list)(list_keys, hot_all)
    drawn = drawn.reshape(DEVICES, TABLES, B_DEV, BAG).transpose(0, 2, 1, 3)
    return drawn.reshape(DEVICES * B_DEV, TABLES, BAG).astype(jnp.int32)


def set_ends(values, key, low, top_value):
    extent = values.shape
    place = [jax.random.randint(jax.random.fold_in(key, axis), (), 0, extent[axis]) for axis in range(len(extent))]
    values = values.at[tuple(place)].set(low)
    longest = extent.index(max(extent))
    place[longest] = (place[longest] + 1) % extent[longest]
    return values.at[tuple(place)].set(top_value)


def raised(result, own_key, source, target, parts, factor):
    owner, partner = [(jnp.arange(result.shape[axis_at]) // (result.shape[axis_at] // parts)).reshape([-1 if axis == axis_at else 1 for axis in range(result.ndim)]) for axis_at in (source, target)]
    chosen = jax.random.permutation(own_key, parts)[partner]
    strong = (owner == chosen) | (owner == (partner + parts // 2) % parts)
    return jnp.where(strong, factor * result, result)


def block_levels(stream_key, dims, shards, smallest, top_value):
    def one(dim, shards_of):
        heights = jax.random.uniform(jax.random.fold_in(jax.random.fold_in(stream_key, 6), dim), (shards_of,), jnp.float32, smallest / len(shards), top_value / len(shards))
        return jnp.repeat(jnp.exp(heights), dims[dim] // shards_of).reshape((-1,) + (1,) * (len(dims) - dim - 1))

    gain = one(*shards[0])
    for cut in shards[1:]:
        gain = gain * one(*cut)
    return gain


def rank_bounds(number_of, slope):
    loads = [(1 << 20) // math.isqrt(standing ** slope) + 1 for standing in range(1, number_of + 1)]
    width = 1 + sum(loads) // (1 << 30)
    return np.cumsum(np.array([max(1, weight // width) for weight in loads]))


def ranked(own_key, extent, amount, skew):
    listing = rank_bounds(amount, skew)
    ticket = jax.random.randint(jax.random.fold_in(own_key, 1), extent, 0, int(listing[amount - 1]))
    standing = jnp.searchsorted(jnp.asarray(listing, jnp.int32), ticket, side="right")
    return jax.random.permutation(jax.random.fold_in(own_key, 2), amount)[standing].astype(jnp.int32)


def noise(key, shape, scale, reach, shards=(), kind=jnp.bfloat16):
    gain = block_levels(key, shape, shards, -0.22, 0.18) if shards else 1.0
    values = jax.random.normal(key, shape, jnp.float32) * scale * gain
    return jnp.minimum(jnp.maximum(values, -reach), reach).astype(kind)


def bell_draw_with(rng, extent, deviation, reach, pieces, heavy, held_as=jnp.bfloat16):
    values = deviation * jax.random.normal(rng, extent, jnp.float32)
    if pieces:
        values = values * block_levels(rng, extent, pieces, -0.22, 0.18)
    return jnp.clip(raised(values, jax.random.fold_in(rng, 3), *heavy), -reach, reach).astype(held_as)


def setup_inputs(seed: int = 0) -> dict:
    splits = jax.random.split(jax.random.key(seed), 9)
    return {
        "bottom_in": noise(splits[0], (BATCH, BOT_IN), 1.0, 6.0, ((0, 32),)),
        "bottom_pre": noise(splits[1], (BATCH, D), 1.0, 6.0, ((0, 32),)),
        "pooled": noise(splits[2], (BATCH, TABLES, D), 1.0, 6.0, ((0, 32),)),
        "top_pre": noise(splits[3], (BATCH, TOP), 1.0, 6.0, ((0, 32),)),
        "top_cotangent": bell_draw_with(splits[4], (BATCH, TOP), TOP ** -0.5, 0.375, ((0, 32),), (0, 1, 32, 2.75)),
        "top_weight": noise(splits[5], (TOP_IN, TOP), D ** -0.5, 0.5),
        "lookup_owner": draw_lookup_owner(jax.random.fold_in(splits[8], 71), 0),
        "lookup_row": set_ends(ranked(splits[7], (BATCH, TABLES, BAG), ROWS_DEV, 2), jax.random.fold_in(splits[7], 3), 0, ROWS_DEV - 1).astype(jnp.int32),
    }


def table_gradient(bag_grad, lookup_owner, lookup_row):
    slot_total = TABLES * ROWS
    accum = jnp.zeros((slot_total, D), jnp.float32)
    table_ids = jnp.arange(TABLES, dtype=jnp.int32)[None, :, None]

    def add_block(block, accum):
        start = (block * B_DEV).astype(jnp.int32)
        grads = lax.dynamic_slice_in_dim(bag_grad, start, B_DEV, 0)
        owners = lax.dynamic_slice_in_dim(lookup_owner, start, B_DEV, 0)
        rows_here = lax.dynamic_slice_in_dim(lookup_row, start, B_DEV, 0)
        target = table_ids * ROWS + owners * ROWS_DEV + rows_here
        values = jnp.broadcast_to(grads[:, :, None, :], (B_DEV, TABLES, BAG, D)).astype(jnp.float32)
        return accum.at[target.reshape(-1)].add(values.reshape(-1, D))

    accum = lax.fori_loop(0, BATCH // B_DEV, add_block, accum)
    return accum.reshape(TABLES, ROWS, D)


def reference(bottom_in, bottom_pre, pooled, top_pre, top_cotangent, top_weight, lookup_owner, lookup_row):
    top_grad = jnp.where(top_pre > 0, top_cotangent, jnp.zeros_like(top_cotangent))
    bottom_out = jnp.maximum(bottom_pre, jnp.zeros_like(bottom_pre))
    feature = jnp.concatenate([bottom_out, pooled.reshape(BATCH, TABLES * D)], axis=1)
    top_weight_grad = lax.dot_general(feature, top_grad, (((0,), (0,)), ((), ())), preferred_element_type=jnp.float32)
    top_bias_grad = jnp.sum(top_grad.astype(jnp.float32), axis=0)
    feature_grad = lax.dot_general(top_grad, top_weight, (((1,), (1,)), ((), ())), preferred_element_type=jnp.float32).astype(jnp.bfloat16)
    bottom_grad = jnp.where(bottom_pre > 0, feature_grad[:, :D], jnp.zeros_like(bottom_pre))
    bottom_weight_grad = lax.dot_general(bottom_in, bottom_grad, (((0,), (0,)), ((), ())), preferred_element_type=jnp.float32)
    bag_grad = feature_grad[:, D:].reshape(BATCH, TABLES, D)
    table_grad = table_gradient(bag_grad, lookup_owner, lookup_row)
    return table_grad, top_weight_grad, top_bias_grad, bottom_weight_grad
```

```python
import functools

import jax
import jax.numpy as jnp
from jax import lax
from jax.experimental import pallas as pl
from jax.experimental.pallas import tpu as pltpu
from jax.sharding import PartitionSpec as P

ROWS_DEV = 2048
LOW = 256
BAG_STEP = 4096
ROW_BLOCK = 512
AXES = ("gx", "gy")


def one_hot(condition):
    return jnp.where(condition, 1.0, 0.0).astype(jnp.bfloat16)


def pack_kernel(devices, capacity, tables, owner_ref, row_ref, codes_ref):
    lists, bags = owner_ref.shape
    bag_size = lists // tables
    f32 = jnp.float32
    earlier = one_hot(
        lax.broadcasted_iota(jnp.int32, (bags, bags), 0)
        < lax.broadcasted_iota(jnp.int32, (bags, bags), 1)
    )
    owner_ids = lax.broadcasted_iota(jnp.int32, (devices, bags), 0)
    slot_ids = lax.broadcasted_iota(jnp.int32, (capacity, bags), 0)
    bag_ids = lax.broadcasted_iota(jnp.int32, (1, bags), 1).astype(f32)
    for table in range(tables):
        carry = jnp.zeros((devices, 1), f32)
        total = jnp.zeros((3 * devices, capacity), f32)
        for item in range(bag_size):
            at = table * bag_size + item
            owner = owner_ref[at : at + 1, :]
            row = row_ref[at : at + 1, :] + LOW
            hit = owner == owner_ids
            member = jnp.where(hit, 1.0, 0.0)
            before = lax.dot_general(
                member.astype(jnp.bfloat16),
                earlier,
                (((1,), (0,)), ((), ())),
                preferred_element_type=f32,
            )
            slot = jnp.sum(member * (before + carry), axis=0, keepdims=True)
            carry = carry + jnp.sum(member, axis=1, keepdims=True)
            high = (row // LOW).astype(f32)
            low = (row % LOW).astype(f32)
            left = jnp.concatenate(
                [member * bag_ids, member * high, member * low], axis=0
            ).astype(jnp.bfloat16)
            right = one_hot(slot.astype(jnp.int32) == slot_ids)
            total = total + lax.dot_general(
                left, right, (((1,), (1,)), ((), ())), preferred_element_type=f32
            )
        code = total[:devices] * BAG_STEP + total[devices : 2 * devices] * LOW + total[2 * devices :]
        codes_ref[:, table * capacity : (table + 1) * capacity] = code.astype(jnp.int32)


def add_kernel(capacity, tables, bags, width, sub, codes_ref, grads_ref, out_ref):
    f32 = jnp.float32
    group = codes_ref.shape[1]
    local_rows = out_ref.shape[1]
    parts = local_rows // ROW_BLOCK

    @pl.when(pl.program_id(0) == 0)
    def _():
        out_ref[...] = jnp.zeros_like(out_ref)

    codes = codes_ref[0]
    columns = jnp.transpose(codes)
    bag_ids = lax.broadcasted_iota(jnp.int32, (capacity, bags), 1)
    row_ids = lax.broadcasted_iota(jnp.int32, (ROW_BLOCK, capacity), 0)
    for table in range(tables):
        for first in range(0, group, sub):
            lefts, rights = [], []
            for source in range(first, first + sub):
                spot = slice(table * capacity, (table + 1) * capacity)
                line = codes[source : source + 1, spot] % BAG_STEP - LOW
                lefts.append(one_hot((line & (ROW_BLOCK - 1)) == row_ids))
                column = columns[spot, source : source + 1]
                picked = lax.dot_general(
                    one_hot((column // BAG_STEP) == bag_ids),
                    grads_ref[source * bags : (source + 1) * bags, table * width : (table + 1) * width],
                    (((1,), (0,)), ((), ())),
                    preferred_element_type=f32,
                )
                part = jnp.broadcast_to((column % BAG_STEP - LOW) // ROW_BLOCK, picked.shape)
                rights.append(
                    jnp.concatenate(
                        [jnp.where(part == p, picked, 0.0).astype(jnp.bfloat16) for p in range(parts)],
                        axis=1,
                    )
                )
            result = lax.dot_general(
                jnp.concatenate(lefts, axis=1),
                jnp.concatenate(rights, axis=0),
                (((1,), (0,)), ((), ())),
                preferred_element_type=f32,
            )
            for p in range(parts):
                out_ref[table, p * ROW_BLOCK : (p + 1) * ROW_BLOCK, :] += result[
                    :, p * width : (p + 1) * width
                ]


def pack_codes(owner_lists, row_lists, devices, capacity, tables):
    return pl.pallas_call(
        functools.partial(pack_kernel, devices, capacity, tables),
        out_shape=jax.ShapeDtypeStruct((devices, tables * capacity), jnp.int32),
        in_specs=[pl.BlockSpec(memory_space=pltpu.VMEM)] * 2,
        out_specs=pl.BlockSpec(memory_space=pltpu.VMEM),
        compiler_params=pltpu.CompilerParams(vmem_limit_bytes=32 * 2**20),
        cost_estimate=pl.CostEstimate(flops=2 * 10**9, bytes_accessed=10**6, transcendentals=0),
        name="pack",
    )(owner_lists, row_lists)


def add_rows(codes, grads, capacity, tables, bags, width, local_rows):
    sources = codes.shape[0]
    group = 8
    steps = sources // group
    return pl.pallas_call(
        functools.partial(add_kernel, capacity, tables, bags, width, 4),
        grid=(steps,),
        out_shape=jax.ShapeDtypeStruct((tables, local_rows, width), jnp.float32),
        in_specs=[
            pl.BlockSpec((1, group, tables * capacity), lambda i: (i, 0, 0)),
            pl.BlockSpec((group * bags, tables * width), lambda i: (i, 0)),
        ],
        out_specs=pl.BlockSpec((tables, local_rows, width), lambda i: (0, 0, 0)),
        compiler_params=pltpu.CompilerParams(vmem_limit_bytes=48 * 2**20),
        cost_estimate=pl.CostEstimate(flops=40 * 10**9, bytes_accessed=8 * 10**6, transcendentals=0),
        name="add_rows",
    )(codes.reshape(steps, group, tables * capacity), grads)


def shards(
    bottom_in, bottom_pre, pooled, top_pre, top_cotangent, top_weight, lookup_owner, lookup_row
):
    bags = bottom_in.shape[0]
    tables = pooled.shape[1]
    width = pooled.shape[2]
    bag_size = lookup_owner.shape[2]
    devices = lax.axis_size("gx") * lax.axis_size("gy")
    capacity = max(2, 2 * bags * bag_size // devices)
    top_grad = jnp.where(top_pre > 0, top_cotangent, jnp.zeros_like(top_cotangent))
    feature_grad = lax.dot_general(
        top_grad, top_weight, (((1,), (1,)), ((), ())), preferred_element_type=jnp.float32
    ).astype(jnp.bfloat16)
    grads = lax.all_gather(feature_grad[:, width:], AXES, axis=0, tiled=True)
    owner_lists = lookup_owner.reshape(bags, tables * bag_size).T
    row_lists = lookup_row.reshape(bags, tables * bag_size).T
    codes = pack_codes(owner_lists, row_lists, devices, capacity, tables)
    codes = lax.all_to_all(codes, AXES, split_axis=0, concat_axis=0, tiled=True)
    bottom_out = jnp.maximum(bottom_pre, jnp.zeros_like(bottom_pre))
    feature = jnp.concatenate([bottom_out, pooled.reshape(bags, tables * width)], axis=1)
    top_weight_part = lax.dot_general(
        feature, top_grad, (((0,), (0,)), ((), ())), preferred_element_type=jnp.float32
    )
    top_bias_part = jnp.sum(top_grad.astype(jnp.float32), axis=0)
    bottom_grad = jnp.where(bottom_pre > 0, feature_grad[:, :width], jnp.zeros_like(bottom_pre))
    bottom_weight_part = lax.dot_general(
        bottom_in, bottom_grad, (((0,), (0,)), ((), ())), preferred_element_type=jnp.float32
    )
    shares = (
        lax.psum_scatter(top_weight_part, "gy", scatter_dimension=0, tiled=True),
        lax.psum_scatter(top_bias_part, "gy", scatter_dimension=0, tiled=True),
        lax.psum_scatter(bottom_weight_part, "gy", scatter_dimension=0, tiled=True),
    )
    top_weight_grad, top_bias_grad, bottom_weight_grad = lax.psum(shares, "gx")
    table_grad = add_rows(codes, grads, capacity, tables, bags, width, ROWS_DEV)
    return (table_grad, top_weight_grad, top_bias_grad, bottom_weight_grad)


def solution(mesh):
    return jax.shard_map(
        shards,
        mesh=mesh,
        in_specs=(
            P(AXES, None),
            P(AXES, None),
            P(AXES, None, None),
            P(AXES, None),
            P(AXES, None),
            P(),
            P(AXES, None, None),
            P(AXES, None, None),
        ),
        out_specs=(P(None, AXES, None), P("gy", None), P("gy"), P("gy", None)),
        check_vma=False,
    )
```

```python
import functools

import jax
import jax.numpy as jnp
from jax import lax
from jax.experimental import pallas as pl
from jax.experimental.pallas import tpu as pltpu
from jax.sharding import PartitionSpec as P

ROWS_DEV = 2048
LOW = 256
BAG_STEP = 4096
ROW_BLOCK = 512
AXES = ("gx", "gy")


def one_hot(condition):
    return jnp.where(condition, 1.0, 0.0).astype(jnp.bfloat16)


def exchange_kernel(
    gx_count, gy_count, capacity, tables,
    owner_ref, row_ref, own_ref, part_ref,
    grads_ref, codes_ref, sums_ref,
    lists, outgoing, pair_in, pair_sum, plane_in, plane_sum, line_in,
    keep_sem, line_send, plane_send, core_send, block_recv, code_send, code_recv,
    pair_sems, plane_sum_send, plane_sum_recv, line_sum_send, line_sum_recv,
    back_send, back_core_send, back_recv,
):
    chips = gx_count // 2
    devices = gx_count * gy_count
    gx, gy = lax.axis_index("gx"), lax.axis_index("gy")
    me = gx * gy_count + gy
    z, core = gx // 2, gx % 2
    sibling = (z * 2 + 1 - core, gy)
    bags = own_ref.shape[0]
    f32 = jnp.float32

    def remote(source, target, send, recv, device):
        return pltpu.make_async_remote_copy(
            src_ref=source,
            dst_ref=target,
            send_sem=send,
            recv_sem=recv,
            device_id=device,
            device_id_type=pl.DeviceIdType.MESH,
        )

    def loop(low, high, body):
        def step(i, none):
            body(i)
            return none

        lax.fori_loop(low, high, step, 0)

    barrier = pltpu.get_barrier_semaphore()

    def greet(k):
        other = lax.rem(me + k, devices)
        pl.semaphore_signal(
            barrier,
            inc=1,
            device_id=(other // gy_count, lax.rem(other, gy_count)),
            device_id_type=pl.DeviceIdType.MESH,
        )

    loop(1, devices, greet)
    pl.semaphore_wait(barrier, devices - 1)

    def block(z_at, core_at, gy_at):
        return (z_at * 2 + core_at) * gy_count + gy_at

    def chip(k):
        return lax.rem(z + k, chips)

    def plane(k):
        return lax.rem(gy + k, gy_count)

    def along_line(k):
        return remote(
            own_ref, grads_ref.at[me], line_send.at[k], block_recv.at[me],
            (chip(k) * 2 + core, gy),
        )

    def in_plane(k, m):
        at = block(chip(k), core, gy)
        return remote(
            grads_ref.at[at], grads_ref.at[at], plane_send.at[k, m], block_recv.at[at],
            (gx, plane(m)),
        )

    def own_in_plane(m):
        return remote(
            own_ref, grads_ref.at[me], plane_send.at[0, m], block_recv.at[me], (gx, plane(m))
        )

    def to_core(at):
        return remote(
            grads_ref.at[at], grads_ref.at[at], core_send.at[at], block_recv.at[at], sibling
        )

    own_to_core = remote(own_ref, grads_ref.at[me], core_send.at[me], block_recv.at[me], sibling)
    pair = remote(part_ref.at[:, 1 - core], pair_in, pair_sems.at[0], pair_sems.at[1], sibling)
    keep = pltpu.make_async_copy(own_ref, grads_ref.at[me], keep_sem)
    loop(1, chips, lambda k: along_line(k).start())
    pair.start()
    loop(1, gy_count, lambda m: own_in_plane(m).start())
    own_to_core.start()
    keep.start()

    earlier = one_hot(
        lax.broadcasted_iota(jnp.int32, (bags, bags), 0)
        < lax.broadcasted_iota(jnp.int32, (bags, bags), 1)
    )
    owner_ids = lax.broadcasted_iota(jnp.int32, (devices, bags), 0)
    slot_ids = lax.broadcasted_iota(jnp.int32, (capacity, bags), 0)
    bag_ids = lax.broadcasted_iota(jnp.int32, (1, bags), 1).astype(f32)
    bag_size = owner_ref.shape[0] // tables

    def pack(table):
        def item(i, state):
            carry, total = state
            lefts, rights = [], []
            owners = owner_ref[pl.ds(table * bag_size + i * 8, 8), :]
            rows = row_ref[pl.ds(table * bag_size + i * 8, 8), :] + LOW
            highs = (rows // LOW).astype(f32)
            lows = (rows % LOW).astype(f32)
            for k in range(8):
                member = jnp.where(owners[k : k + 1] == owner_ids, 1.0, 0.0)
                before = lax.dot_general(
                    member.astype(jnp.bfloat16),
                    earlier,
                    (((1,), (0,)), ((), ())),
                    preferred_element_type=f32,
                )
                slot = jnp.sum(member * (before + carry), axis=0, keepdims=True)
                carry = carry + jnp.sum(member, axis=1, keepdims=True)
                lefts.append(
                    jnp.concatenate(
                        [member * bag_ids, member * highs[k : k + 1], member * lows[k : k + 1]],
                        axis=0,
                    ).astype(jnp.bfloat16)
                )
                rights.append(one_hot(slot.astype(jnp.int32) == slot_ids))
            total = total + lax.dot_general(
                jnp.concatenate(lefts, axis=1),
                jnp.concatenate(rights, axis=1),
                (((1,), (1,)), ((), ())),
                preferred_element_type=f32,
            )
            return carry, total

        _, total = lax.fori_loop(
            0,
            bag_size // 8,
            item,
            (jnp.zeros((devices, 1), f32), jnp.zeros((3 * devices, capacity), f32)),
        )
        code = total[:devices] * BAG_STEP + total[devices : 2 * devices] * LOW + total[2 * devices :]
        lists[:, table * capacity : (table + 1) * capacity] = code.astype(jnp.int32)

    pack(0)

    pair.wait_recv()

    def pair_add(g):
        pair_sum[g] = part_ref[g, core] + pair_in[g]

    loop(0, gy_count, pair_add)

    def plane_sums(m):
        return remote(
            pair_sum.at[plane(m)], plane_in.at[gy], plane_sum_send.at[m], plane_sum_recv.at[gy],
            (gx, plane(m)),
        )

    loop(1, gy_count, lambda m: plane_sums(m).start())

    def forward_line(k):
        at = block(chip(k), core, gy)
        to_core(at).wait_recv()
        loop(1, gy_count, lambda m: in_plane(k, m).start())
        to_core(at).start()

    loop(1, chips, forward_line)

    for table in range(1, tables):
        pack(table)
    lines = outgoing.shape[1]
    for k in range(lines):
        outgoing[:, k, :] = lists[:, k * 128 : (k + 1) * 128]
    codes_ref[me] = outgoing[me]

    def code_to(k):
        other = lax.rem(me + k, devices)
        return remote(
            outgoing.at[other], codes_ref.at[me], code_send.at[k], code_recv.at[me],
            (other // gy_count, lax.rem(other, gy_count)),
        )

    loop(1, devices, lambda k: code_to(k).start())

    plane_sum[...] = pair_sum[gy]

    def plane_add(m):
        at = plane(m)
        remote(
            plane_in.at[at], plane_in.at[at], plane_sum_send.at[m], plane_sum_recv.at[at], sibling
        ).wait_recv()
        plane_sum[...] += plane_in[at]

    loop(1, gy_count, plane_add)

    def line_sums(k):
        return remote(
            plane_sum.at[chip(k)], line_in.at[z], line_sum_send.at[k], line_sum_recv.at[z],
            (chip(k) * 2 + core, gy),
        )

    loop(1, chips, lambda k: line_sums(k).start())

    def forward_plane(m):
        def one(k):
            at = block(chip(k), core, plane(m))
            to_core(at).wait_recv()
            to_core(at).start()

        loop(0, chips, one)

    loop(1, gy_count, forward_plane)

    sums_ref[core, z] = plane_sum[z]

    def line_add(k):
        at = chip(k)
        remote(
            line_in.at[at], line_in.at[at], line_sum_send.at[k], line_sum_recv.at[at], sibling
        ).wait_recv()
        sums_ref[core, z] += line_in[at]

    loop(1, chips, line_add)

    def back(k):
        return remote(
            sums_ref.at[core, z], sums_ref.at[core, z], back_send.at[k], back_recv.at[core, z],
            (chip(k) * 2 + core, gy),
        )

    def back_core(k):
        at = chip(k)
        return remote(
            sums_ref.at[core, at], sums_ref.at[core, at], back_core_send.at[k],
            back_recv.at[core, at], sibling,
        )

    def back_arrived(core_at, at):
        return remote(
            sums_ref.at[core_at, at], sums_ref.at[core_at, at], back_core_send.at[0],
            back_recv.at[core_at, at], sibling,
        )

    loop(1, chips, lambda k: back(k).start())
    back_core(0).start()

    def forward_back(k):
        back_arrived(core, chip(k)).wait_recv()
        back_core(k).start()

    loop(1, chips, forward_back)

    def code_arrived(k):
        at = lax.rem(me + k, devices)
        remote(
            codes_ref.at[at], codes_ref.at[at], code_send.at[k], code_recv.at[at], sibling
        ).wait_recv()

    loop(1, devices, code_arrived)
    loop(0, chips, lambda k: back_arrived(1 - core, k).wait_recv())

    def core_arrived(k):
        loop(0, gy_count, lambda g: to_core(block(k, 1 - core, g)).wait_recv())

    loop(0, chips, core_arrived)
    keep.wait()
    pair.wait_send()
    own_to_core.wait_send()
    loop(1, chips, lambda k: along_line(k).wait_send())
    loop(1, gy_count, lambda m: own_in_plane(m).wait_send())
    loop(1, chips, lambda k: loop(1, gy_count, lambda m: in_plane(k, m).wait_send()))
    loop(1, chips, lambda k: to_core(block(chip(k), core, gy)).wait_send())
    loop(
        1,
        gy_count,
        lambda m: loop(0, chips, lambda k: to_core(block(chip(k), core, plane(m))).wait_send()),
    )
    loop(1, gy_count, lambda m: plane_sums(m).wait_send())
    loop(1, chips, lambda k: line_sums(k).wait_send())
    loop(1, chips, lambda k: back(k).wait_send())
    loop(0, chips, lambda k: back_core(k).wait_send())
    loop(1, devices, lambda k: code_to(k).wait_send())


def add_kernel(capacity, tables, bags, width, sub, codes_ref, grads_ref, out_ref):
    f32 = jnp.float32
    group = codes_ref.shape[1]
    local_rows = out_ref.shape[1]
    parts = local_rows // ROW_BLOCK

    @pl.when(pl.program_id(0) == 0)
    def _():
        out_ref[...] = jnp.zeros_like(out_ref)

    codes = codes_ref[0]
    columns = jnp.transpose(codes)
    bag_ids = lax.broadcasted_iota(jnp.int32, (capacity, bags), 1)
    row_ids = lax.broadcasted_iota(jnp.int32, (ROW_BLOCK, capacity), 0)
    for table in range(tables):
        for first in range(0, group, sub):
            lefts, rights = [], []
            for source in range(first, first + sub):
                spot = slice(table * capacity, (table + 1) * capacity)
                line = codes[source : source + 1, spot] % BAG_STEP - LOW
                lefts.append(one_hot((line & (ROW_BLOCK - 1)) == row_ids))
                column = columns[spot, source : source + 1]
                picked = lax.dot_general(
                    one_hot((column // BAG_STEP) == bag_ids),
                    grads_ref[source * bags : (source + 1) * bags, table * width : (table + 1) * width],
                    (((1,), (0,)), ((), ())),
                    preferred_element_type=f32,
                )
                part = jnp.broadcast_to((column % BAG_STEP - LOW) // ROW_BLOCK, picked.shape)
                rights.append(
                    jnp.concatenate(
                        [jnp.where(part == p, picked, 0.0).astype(jnp.bfloat16) for p in range(parts)],
                        axis=1,
                    )
                )
            result = lax.dot_general(
                jnp.concatenate(lefts, axis=1),
                jnp.concatenate(rights, axis=0),
                (((1,), (0,)), ((), ())),
                preferred_element_type=f32,
            )
            for p in range(parts):
                out_ref[table, p * ROW_BLOCK : (p + 1) * ROW_BLOCK, :] += result[
                    :, p * width : (p + 1) * width
                ]


def exchange(owner_lists, row_lists, own, part, gx_count, gy_count, capacity, tables):
    devices = gx_count * gy_count
    chips = gx_count // 2
    bags, both = own.shape
    q, columns = part.shape[3:]
    lines = tables * capacity // 128
    f32 = jnp.float32
    vmem = pl.BlockSpec(memory_space=pltpu.VMEM)
    dma = pltpu.SemaphoreType.DMA
    return pl.pallas_call(
        functools.partial(exchange_kernel, gx_count, gy_count, capacity, tables),
        out_shape=(
            jax.ShapeDtypeStruct((devices, bags, both), jnp.bfloat16),
            jax.ShapeDtypeStruct((devices, lines, 128), jnp.int32),
            jax.ShapeDtypeStruct((2, chips, q, columns), f32),
        ),
        in_specs=[vmem] * 4,
        out_specs=(pl.BlockSpec(memory_space=pl.ANY), vmem, vmem),
        scratch_shapes=[
            pltpu.VMEM((devices, tables * capacity), jnp.int32),
            pltpu.VMEM((devices, lines, 128), jnp.int32),
            pltpu.VMEM((gy_count, chips, q, columns), f32),
            pltpu.VMEM((gy_count, chips, q, columns), f32),
            pltpu.VMEM((gy_count, chips, q, columns), f32),
            pltpu.VMEM((chips, q, columns), f32),
            pltpu.VMEM((chips, q, columns), f32),
            dma(()),
            dma((chips,)),
            dma((chips, gy_count)),
            dma((devices,)),
            dma((devices,)),
            dma((devices,)),
            dma((devices,)),
            dma((2,)),
            dma((gy_count,)),
            dma((gy_count,)),
            dma((chips,)),
            dma((chips,)),
            dma((chips,)),
            dma((chips,)),
            dma((2, chips)),
        ],
        compiler_params=pltpu.CompilerParams(
            vmem_limit_bytes=48 * 2**20, collective_id=0, has_side_effects=True
        ),
        cost_estimate=pl.CostEstimate(flops=2 * 10**9, bytes_accessed=10**7, transcendentals=0),
        name="exchange",
    )(owner_lists, row_lists, own, part)


def add_rows(codes, grads, capacity, tables, bags, width, local_rows):
    sources = codes.shape[0]
    group = 8
    steps = sources // group
    return pl.pallas_call(
        functools.partial(add_kernel, capacity, tables, bags, width, 4),
        grid=(steps,),
        out_shape=jax.ShapeDtypeStruct((tables, local_rows, width), jnp.float32),
        in_specs=[
            pl.BlockSpec((1, group, tables * capacity), lambda i: (i, 0, 0)),
            pl.BlockSpec((group * bags, tables * width), lambda i: (i, 0)),
        ],
        out_specs=pl.BlockSpec((tables, local_rows, width), lambda i: (0, 0, 0)),
        compiler_params=pltpu.CompilerParams(vmem_limit_bytes=48 * 2**20),
        cost_estimate=pl.CostEstimate(flops=40 * 10**9, bytes_accessed=8 * 10**6, transcendentals=0),
        name="add_rows",
    )(codes.reshape(steps, group, tables * capacity), grads)


def shards(
    bottom_in, bottom_pre, pooled, top_pre, top_cotangent, top_weight, lookup_owner, lookup_row
):
    bags = bottom_in.shape[0]
    tables = pooled.shape[1]
    width = pooled.shape[2]
    bag_size = lookup_owner.shape[2]
    gx_count, gy_count = lax.axis_size("gx"), lax.axis_size("gy")
    devices = gx_count * gy_count
    capacity = max(2, 2 * bags * bag_size // devices)
    f32 = jnp.float32
    top_grad = jnp.where(top_pre > 0, top_cotangent, jnp.zeros_like(top_cotangent))
    feature_grad = lax.dot_general(
        top_grad, top_weight, (((1,), (1,)), ((), ())), preferred_element_type=f32
    ).astype(jnp.bfloat16)
    owner_lists = lookup_owner.reshape(bags, tables * bag_size).T
    row_lists = lookup_row.reshape(bags, tables * bag_size).T
    bottom_out = jnp.maximum(bottom_pre, jnp.zeros_like(bottom_pre))
    feature = jnp.concatenate([bottom_out, pooled.reshape(bags, tables * width)], axis=1)
    top_weight_part = lax.dot_general(
        feature, top_grad, (((0,), (0,)), ((), ())), preferred_element_type=f32
    )
    top_bias_part = jnp.sum(top_grad.astype(f32), axis=0)
    bottom_grad = jnp.where(bottom_pre > 0, feature_grad[:, :width], jnp.zeros_like(bottom_pre))
    bottom_weight_part = lax.dot_general(
        bottom_in, bottom_grad, (((0,), (0,)), ((), ())), preferred_element_type=f32
    )
    columns = top_weight_part.shape[1]
    top_rows = top_weight_part.shape[0] // gy_count
    bottom_rows = bottom_weight_part.shape[0] // gy_count
    bias_share = columns // gy_count
    bottom_lines = bottom_rows * width // columns
    used = top_rows + bottom_lines + 1
    q = -(-used // (gx_count * 8)) * 8
    bias_lines = jnp.pad(
        top_bias_part.reshape(gy_count, 1, bias_share),
        ((0, 0), (0, gx_count * q - used), (0, columns - bias_share)),
    )
    part = jnp.concatenate(
        [
            top_weight_part.reshape(gy_count, top_rows, columns),
            bottom_weight_part.reshape(gy_count, bottom_lines, columns),
            bias_lines,
        ],
        axis=1,
    ).reshape(gy_count, 2, gx_count // 2, q, columns)
    grads, codes, sums = exchange(
        owner_lists, row_lists, feature_grad[:, width:], part, gx_count, gy_count, capacity, tables
    )
    sums = sums.reshape(gx_count * q, columns)
    top_weight_grad = sums[:top_rows]
    bottom_weight_grad = sums[top_rows : top_rows + bottom_lines].reshape(bottom_rows, width)
    top_bias_grad = sums[top_rows + bottom_lines, :bias_share]
    codes = codes.reshape(devices, tables * capacity)
    grads = grads.reshape(devices * bags, tables * width)
    table_grad = add_rows(codes, grads, capacity, tables, bags, width, ROWS_DEV)
    return (table_grad, top_weight_grad, top_bias_grad, bottom_weight_grad)


def solution(mesh):
    return jax.shard_map(
        shards,
        mesh=mesh,
        in_specs=(
            P(AXES, None),
            P(AXES, None),
            P(AXES, None, None),
            P(AXES, None),
            P(AXES, None),
            P(),
            P(AXES, None, None),
            P(AXES, None, None),
        ),
        out_specs=(P(None, AXES, None), P("gy", None), P("gy"), P("gy", None)),
        check_vma=False,
    )
```

```python
import functools

import jax
import jax.numpy as jnp
from jax import lax
from jax.experimental import pallas as pl
from jax.experimental.pallas import tpu as pltpu
from jax.sharding import PartitionSpec as P

ROWS_DEV = 2048
LOW = 256
BAG_STEP = 4096
ROW_BLOCK = 512
AXES = ("gx", "gy")


def one_hot(left, right):
    one = jnp.ones((), jnp.bfloat16)
    return jnp.where(left == right, one, jnp.zeros((), jnp.bfloat16))


def count(shape, axis, less=0):
    numbers = lax.broadcasted_iota(jnp.int32, shape, axis) - less
    return numbers.astype(jnp.float32).astype(jnp.bfloat16)


def exchange_kernel(
    gx_count, gy_count, capacity, tables,
    owner_ref, row_ref, own_ref, part_ref,
    table_ref, sums_ref,
    grads_ref, codes_ref, lists, outgoing, pair_in, pair_sum, plane_in, plane_sum, line_in,
    keep_sem, line_send, plane_send, core_send, block_recv, code_send, code_recv,
    pair_sems, plane_sum_send, plane_sum_recv, line_sum_send, line_sum_recv,
    back_send, back_core_send, back_recv,
):
    chips = gx_count // 2
    devices = gx_count * gy_count
    gx, gy = lax.axis_index("gx"), lax.axis_index("gy")
    me = gx * gy_count + gy
    z, core = gx // 2, gx % 2
    sibling = (z * 2 + 1 - core, gy)
    bags = own_ref.shape[0]
    f32 = jnp.float32

    def remote(source, target, send, recv, device):
        return pltpu.make_async_remote_copy(
            src_ref=source,
            dst_ref=target,
            send_sem=send,
            recv_sem=recv,
            device_id=device,
            device_id_type=pl.DeviceIdType.MESH,
        )

    def loop(low, high, body):
        def step(i, none):
            body(i)
            return none

        lax.fori_loop(low, high, step, 0)

    barrier = pltpu.get_barrier_semaphore()

    def greet(k):
        other = lax.rem(me + k, devices)
        pl.semaphore_signal(
            barrier,
            inc=1,
            device_id=(other // gy_count, lax.rem(other, gy_count)),
            device_id_type=pl.DeviceIdType.MESH,
        )

    loop(1, devices, greet)
    pl.semaphore_wait(barrier, devices - 1)

    def block(z_at, core_at, gy_at):
        return (z_at * 2 + core_at) * gy_count + gy_at

    def chip(k):
        return lax.rem(z + k, chips)

    def plane(k):
        return lax.rem(gy + k, gy_count)

    def along_line(k):
        return remote(
            own_ref, grads_ref.at[me], line_send.at[k], block_recv.at[me],
            (chip(k) * 2 + core, gy),
        )

    def in_plane(k, m):
        at = block(chip(k), core, gy)
        return remote(
            grads_ref.at[at], grads_ref.at[at], plane_send.at[k, m], block_recv.at[at],
            (gx, plane(m)),
        )

    def own_in_plane(m):
        return remote(
            own_ref, grads_ref.at[me], plane_send.at[0, m], block_recv.at[me], (gx, plane(m))
        )

    def to_core(at):
        return remote(
            grads_ref.at[at], grads_ref.at[at], core_send.at[at], block_recv.at[at], sibling
        )

    own_to_core = remote(own_ref, grads_ref.at[me], core_send.at[me], block_recv.at[me], sibling)
    pair = remote(part_ref.at[:, 1 - core], pair_in, pair_sems.at[0], pair_sems.at[1], sibling)
    keep = pltpu.make_async_copy(own_ref, grads_ref.at[me], keep_sem)
    loop(1, chips, lambda k: along_line(k).start())
    pair.start()
    loop(1, gy_count, lambda m: own_in_plane(m).start())
    own_to_core.start()
    keep.start()

    half = capacity // 2
    bf16 = jnp.bfloat16
    earlier = jnp.where(
        lax.broadcasted_iota(jnp.int32, (bags, bags), 0)
        < lax.broadcasted_iota(jnp.int32, (bags, bags), 1),
        1.0,
        0.0,
    ).astype(bf16)
    owner_ids = count((devices, bags), 0)
    slot_ids = count((capacity, bags), 0, half)
    bag_line = count((1, bags), 1)
    nothing = jnp.zeros((), bf16)
    bag_size = owner_ref.shape[0] // tables

    def pack(table):
        def item(i, state):
            carry, total = state
            lefts, rights = [], []
            owners = owner_ref[pl.ds(table * bag_size + i * 8, 8), :].astype(f32)
            rows = row_ref[pl.ds(table * bag_size + i * 8, 8), :] + LOW
            highs = (rows // LOW).astype(f32)
            lows = (rows % LOW).astype(f32)
            for k in range(8):
                hit = owners[k : k + 1].astype(bf16) == owner_ids
                member = jnp.where(hit, jnp.ones((), bf16), nothing)
                before = lax.dot_general(
                    member, earlier, (((1,), (0,)), ((), ())), preferred_element_type=f32
                )
                wide = member.astype(f32)
                slot = jnp.sum(wide * (before + carry), axis=0, keepdims=True)
                carry = carry + jnp.sum(wide, axis=1, keepdims=True)
                lefts.append(
                    jnp.concatenate(
                        [
                            member * bag_line,
                            member * highs[k : k + 1].astype(bf16),
                            member * lows[k : k + 1].astype(bf16),
                        ],
                        axis=0,
                    )
                )
                rights.append(one_hot((slot - half).astype(bf16), slot_ids))
            total = total + lax.dot_general(
                jnp.concatenate(lefts, axis=1),
                jnp.concatenate(rights, axis=1),
                (((1,), (1,)), ((), ())),
                preferred_element_type=f32,
            )
            return carry, total

        _, total = lax.fori_loop(
            0,
            bag_size // 8,
            item,
            (jnp.zeros((devices, 1), f32), jnp.zeros((3 * devices, capacity), f32)),
        )
        code = total[:devices] * BAG_STEP + total[devices : 2 * devices] * LOW + total[2 * devices :]
        lists[:, table * capacity : (table + 1) * capacity] = code.astype(jnp.int32)

    pack(0)

    pair.wait_recv()

    def pair_add(g):
        pair_sum[g] = part_ref[g, core] + pair_in[g]

    loop(0, gy_count, pair_add)

    def plane_sums(m):
        return remote(
            pair_sum.at[plane(m)], plane_in.at[gy], plane_sum_send.at[m], plane_sum_recv.at[gy],
            (gx, plane(m)),
        )

    loop(1, gy_count, lambda m: plane_sums(m).start())

    def forward_line(k):
        at = block(chip(k), core, gy)
        to_core(at).wait_recv()
        loop(1, gy_count, lambda m: in_plane(k, m).start())
        to_core(at).start()

    loop(1, chips, forward_line)

    for table in range(1, tables):
        pack(table)
    lines = outgoing.shape[1]
    for k in range(lines):
        outgoing[:, k, :] = lists[:, k * 128 : (k + 1) * 128]
    codes_ref[me] = outgoing[me]

    def code_to(k):
        other = lax.rem(me + k, devices)
        return remote(
            outgoing.at[other], codes_ref.at[me], code_send.at[k], code_recv.at[me],
            (other // gy_count, lax.rem(other, gy_count)),
        )

    loop(1, devices, lambda k: code_to(k).start())

    def code_arrived(at):
        remote(
            codes_ref.at[at], codes_ref.at[at], code_send.at[0], code_recv.at[at], sibling
        ).wait_recv()

    table_ref[...] = jnp.zeros_like(table_ref)
    parts = table_ref.shape[1] // ROW_BLOCK
    width = table_ref.shape[2]
    piece = min(capacity, 128)
    pieces = capacity // piece
    bag_ids = count((piece, bags), 1)
    row_ids = count((ROW_BLOCK, capacity), 0, ROW_BLOCK // 2)

    def add_unit(core_at, gy_at):
        lefts = [[] for _ in range(tables)]
        rights = [[] for _ in range(tables)]
        for k in range(chips):
            at = block(chip(k), core_at, gy_at)
            codes = codes_ref[at]
            if lines % 8:
                codes = jnp.broadcast_to(codes[:1], (8, 128))
            row_form = codes % BAG_STEP - LOW
            row_low = ((row_form & (ROW_BLOCK - 1)) - ROW_BLOCK // 2).astype(f32)
            row_part = jnp.transpose((row_form >> (ROW_BLOCK.bit_length() - 1)).astype(f32))
            bag_form = jnp.transpose((codes // BAG_STEP).astype(f32))
            for table in range(tables):
                low_pieces, picked_pieces, part_pieces = [], [], []
                for p in range(pieces):
                    spot = table * capacity + p * piece
                    line, lane = spot // 128, spot % 128
                    low_pieces.append(row_low[line : line + 1, lane : lane + piece])
                    bag = bag_form[lane : lane + piece, line : line + 1]
                    picked_pieces.append(
                        one_hot(jnp.broadcast_to(bag, (piece, bags)).astype(bf16), bag_ids)
                    )
                    part = row_part[lane : lane + piece, line : line + 1]
                    part_pieces.append(jnp.broadcast_to(part, (piece, width)).astype(bf16))
                low = jnp.concatenate(low_pieces, axis=1).astype(bf16)
                lefts[table].append(one_hot(low, row_ids))
                picked = lax.dot_general(
                    jnp.concatenate(picked_pieces, axis=0),
                    grads_ref[at, :, table * width : (table + 1) * width],
                    (((1,), (0,)), ((), ())),
                    preferred_element_type=f32,
                ).astype(bf16)
                part = jnp.concatenate(part_pieces, axis=0)
                rights[table].append(
                    jnp.concatenate(
                        [
                            jnp.where(part == jnp.full((), p, bf16), picked, nothing)
                            for p in range(parts)
                        ],
                        axis=1,
                    )
                )
        for table in range(tables):
            result = lax.dot_general(
                jnp.concatenate(lefts[table], axis=1),
                jnp.concatenate(rights[table], axis=0),
                (((1,), (0,)), ((), ())),
                preferred_element_type=f32,
            )
            for p in range(parts):
                table_ref[table, p * ROW_BLOCK : (p + 1) * ROW_BLOCK, :] += result[
                    :, p * width : (p + 1) * width
                ]

    plane_sum[...] = pair_sum[gy]

    def plane_add(m):
        at = plane(m)
        remote(
            plane_in.at[at], plane_in.at[at], plane_sum_send.at[m], plane_sum_recv.at[at], sibling
        ).wait_recv()
        plane_sum[...] += plane_in[at]

    loop(1, gy_count, plane_add)

    def line_sums(k):
        return remote(
            plane_sum.at[chip(k)], line_in.at[z], line_sum_send.at[k], line_sum_recv.at[z],
            (chip(k) * 2 + core, gy),
        )

    loop(1, chips, lambda k: line_sums(k).start())

    keep.wait()

    def forward_plane(m):
        def one(k):
            at = block(chip(k), core, plane(m))
            to_core(at).wait_recv()
            to_core(at).start()

        loop(0, chips, one)

    loop(1, chips, lambda k: code_arrived(block(chip(k), core, gy)))

    def own_core_unit(m):
        @pl.when(m < gy_count - 1)
        def _():
            forward_plane(m + 1)

        @pl.when(m > 0)
        def _():
            loop(0, chips, lambda k: code_arrived(block(chip(k), core, plane(m))))

        add_unit(core, plane(m))

    loop(0, gy_count, own_core_unit)

    sums_ref[core, z] = plane_sum[z]

    def line_add(k):
        at = chip(k)
        remote(
            line_in.at[at], line_in.at[at], line_sum_send.at[k], line_sum_recv.at[at], sibling
        ).wait_recv()
        sums_ref[core, z] += line_in[at]

    loop(1, chips, line_add)

    def back(k):
        return remote(
            sums_ref.at[core, z], sums_ref.at[core, z], back_send.at[k], back_recv.at[core, z],
            (chip(k) * 2 + core, gy),
        )

    def back_core(k):
        at = chip(k)
        return remote(
            sums_ref.at[core, at], sums_ref.at[core, at], back_core_send.at[k],
            back_recv.at[core, at], sibling,
        )

    def back_arrived(core_at, at):
        return remote(
            sums_ref.at[core_at, at], sums_ref.at[core_at, at], back_core_send.at[0],
            back_recv.at[core_at, at], sibling,
        )

    loop(1, chips, lambda k: back(k).start())
    back_core(0).start()

    def other_core_unit(m):
        def arrive(k):
            at = block(chip(k), 1 - core, plane(m))
            code_arrived(at)
            to_core(at).wait_recv()

        loop(0, chips, arrive)
        add_unit(1 - core, plane(m))

    loop(0, gy_count - 1, other_core_unit)

    def forward_back(k):
        back_arrived(core, chip(k)).wait_recv()
        back_core(k).start()

    loop(1, chips, forward_back)
    other_core_unit(gy_count - 1)

    loop(0, chips, lambda k: back_arrived(1 - core, k).wait_recv())

    pair.wait_send()
    own_to_core.wait_send()
    loop(1, chips, lambda k: along_line(k).wait_send())
    loop(1, gy_count, lambda m: own_in_plane(m).wait_send())
    loop(1, chips, lambda k: loop(1, gy_count, lambda m: in_plane(k, m).wait_send()))
    loop(1, chips, lambda k: to_core(block(chip(k), core, gy)).wait_send())
    loop(
        1,
        gy_count,
        lambda m: loop(0, chips, lambda k: to_core(block(chip(k), core, plane(m))).wait_send()),
    )
    loop(1, gy_count, lambda m: plane_sums(m).wait_send())
    loop(1, chips, lambda k: line_sums(k).wait_send())
    loop(1, chips, lambda k: back(k).wait_send())
    loop(0, chips, lambda k: back_core(k).wait_send())
    loop(1, devices, lambda k: code_to(k).wait_send())


def exchange(owner_lists, row_lists, own, part, gx_count, gy_count, capacity, tables):
    devices = gx_count * gy_count
    chips = gx_count // 2
    bags, both = own.shape
    q, columns = part.shape[3:]
    lines = tables * capacity // 128
    f32 = jnp.float32
    vmem = pl.BlockSpec(memory_space=pltpu.VMEM)
    dma = pltpu.SemaphoreType.DMA
    return pl.pallas_call(
        functools.partial(exchange_kernel, gx_count, gy_count, capacity, tables),
        out_shape=(
            jax.ShapeDtypeStruct((tables, ROWS_DEV, both // tables), f32),
            jax.ShapeDtypeStruct((2, chips, q, columns), f32),
        ),
        in_specs=[vmem] * 4,
        out_specs=(vmem, vmem),
        scratch_shapes=[
            pltpu.VMEM((devices, bags, both), jnp.bfloat16),
            pltpu.VMEM((devices, lines, 128), jnp.int32),
            pltpu.VMEM((devices, tables * capacity), jnp.int32),
            pltpu.VMEM((devices, lines, 128), jnp.int32),
            pltpu.VMEM((gy_count, chips, q, columns), f32),
            pltpu.VMEM((gy_count, chips, q, columns), f32),
            pltpu.VMEM((gy_count, chips, q, columns), f32),
            pltpu.VMEM((chips, q, columns), f32),
            pltpu.VMEM((chips, q, columns), f32),
            dma(()),
            dma((chips,)),
            dma((chips, gy_count)),
            dma((devices,)),
            dma((devices,)),
            dma((devices,)),
            dma((devices,)),
            dma((2,)),
            dma((gy_count,)),
            dma((gy_count,)),
            dma((chips,)),
            dma((chips,)),
            dma((chips,)),
            dma((chips,)),
            dma((2, chips)),
        ],
        compiler_params=pltpu.CompilerParams(
            vmem_limit_bytes=60 * 2**20, collective_id=0, has_side_effects=True
        ),
        cost_estimate=pl.CostEstimate(flops=40 * 10**9, bytes_accessed=10**7, transcendentals=0),
        name="exchange",
    )(owner_lists, row_lists, own, part)


def shards(
    bottom_in, bottom_pre, pooled, top_pre, top_cotangent, top_weight, lookup_owner, lookup_row
):
    bags = bottom_in.shape[0]
    tables = pooled.shape[1]
    width = pooled.shape[2]
    bag_size = lookup_owner.shape[2]
    gx_count, gy_count = lax.axis_size("gx"), lax.axis_size("gy")
    devices = gx_count * gy_count
    capacity = max(2, 2 * bags * bag_size // devices)
    f32 = jnp.float32
    top_grad = jnp.where(top_pre > 0, top_cotangent, jnp.zeros_like(top_cotangent))
    feature_grad = lax.dot_general(
        top_grad, top_weight, (((1,), (1,)), ((), ())), preferred_element_type=f32
    ).astype(jnp.bfloat16)
    owner_lists = lookup_owner.reshape(bags, tables * bag_size).T
    row_lists = lookup_row.reshape(bags, tables * bag_size).T
    bottom_out = jnp.maximum(bottom_pre, jnp.zeros_like(bottom_pre))
    feature = jnp.concatenate([bottom_out, pooled.reshape(bags, tables * width)], axis=1)
    top_weight_part = lax.dot_general(
        feature, top_grad, (((0,), (0,)), ((), ())), preferred_element_type=f32
    )
    top_bias_part = jnp.sum(top_grad.astype(f32), axis=0)
    bottom_grad = jnp.where(bottom_pre > 0, feature_grad[:, :width], jnp.zeros_like(bottom_pre))
    bottom_weight_part = lax.dot_general(
        bottom_in, bottom_grad, (((0,), (0,)), ((), ())), preferred_element_type=f32
    )
    columns = top_weight_part.shape[1]
    top_rows = top_weight_part.shape[0] // gy_count
    bottom_rows = bottom_weight_part.shape[0] // gy_count
    bias_share = columns // gy_count
    bottom_lines = bottom_rows * width // columns
    used = top_rows + bottom_lines + 1
    q = -(-used // (gx_count * 8)) * 8
    bias_lines = jnp.pad(
        top_bias_part.reshape(gy_count, 1, bias_share),
        ((0, 0), (0, gx_count * q - used), (0, columns - bias_share)),
    )
    part = jnp.concatenate(
        [
            top_weight_part.reshape(gy_count, top_rows, columns),
            bottom_weight_part.reshape(gy_count, bottom_lines, columns),
            bias_lines,
        ],
        axis=1,
    ).reshape(gy_count, 2, gx_count // 2, q, columns)
    table_grad, sums = exchange(
        owner_lists, row_lists, feature_grad[:, width:], part, gx_count, gy_count, capacity, tables
    )
    sums = sums.reshape(gx_count * q, columns)
    top_weight_grad = sums[:top_rows]
    bottom_weight_grad = sums[top_rows : top_rows + bottom_lines].reshape(bottom_rows, width)
    top_bias_grad = sums[top_rows + bottom_lines, :bias_share]
    return (table_grad, top_weight_grad, top_bias_grad, bottom_weight_grad)


def solution(mesh):
    return jax.shard_map(
        shards,
        mesh=mesh,
        in_specs=(
            P(AXES, None),
            P(AXES, None),
            P(AXES, None, None),
            P(AXES, None),
            P(AXES, None),
            P(),
            P(AXES, None, None),
            P(AXES, None, None),
        ),
        out_specs=(P(None, AXES, None), P("gy", None), P("gy"), P("gy", None)),
        check_vma=False,
    )
```
